32 devices in a mesh: grp: 2 (over y), bond: 4 (over z), mpo: 2 (over x), sub: 2 (over core).
Axes of the slice: x: 2, y: 2, z: 4, core: 2. Of those that a mesh axis runs over, the one named last changes fastest.
Arguments:
- psi: bfloat16 [2, 192, 128, 128], P(None, ('grp', 'bond'), 'sub'), parts along dimension 1, may hold values from -6 to 6
- left_env: bfloat16 [40, 64, 128, 128], P('mpo', ('grp', 'bond')), parts along dimension 1, may hold values from -0.078125 to 0.078125
- right_env: bfloat16 [40, 64, 128, 128], P('mpo', ('grp', 'bond'), 'sub'), parts along dimension 1, may hold values from -0.5 to 0.5
- left_sector: int32 [192], P(('grp', 'bond')), parts along dimension 0, may hold values from 0 to 7
- right_sector: int32 [192], P(('grp', 'bond')), parts along dimension 0, may hold values from 0 to 7
- dest_device: int32 [192, 1], P(('grp', 'bond')), parts along dimension 0, may hold values from 0 to 3; in each aligned block of 24 rows (0 to 23, 24 to 47, ...) at most 12 rows name the same one
- target_block: int32 [192], P(('grp', 'bond')), parts along dimension 0, may hold values from 0 to 23
- left_size: int32 [64], P(('grp', 'bond')), parts along dimension 0, may hold values from 1 to 128
- right_size: int32 [64], P(('grp', 'bond')), parts along dimension 0, may hold values from 1 to 128
Outputs:
- h_psi: bfloat16 [2, 192, 128, 128], P(None, ('grp', 'bond'), ('mpo', 'sub')), parts along dimension 1
The draws below stay inside these ranges and needn't reach their ends.
There are 2 independent parts, one for each index of `grp`. The reference program is written for one: setup_inputs(seed, part) draws one part's arguments, and reference() takes and returns one part's arrays. A program takes and returns all parts, laid end to end along the dimension named above; each array names one. Nothing has to cross between parts.
Inputs may be any that keep to these rules, and one draw needn't show every extreme that they name: Local indices: left_sector into the sectors of the block's own index of bond, right_sector and target_block into those of its destination. `dest_device`: among the 24 blocks of one index of bond no destination occurs more than 12 times, and some destination occurs exactly 12 times.
All inputs are finite; a program needn't handle non-finite values.
Results may differ from the reference program's by a relative error of at most 0.0049.
Values may be sent and summed in bfloat16 or wider, within the bound.
A program may use at most 256 MiB of HBM per device.

```python
import math
import jax
import jax.numpy as jnp
import numpy as np
from jax import lax

S = 128
W = 40
NB_DEV = 24
NL_DEV = 8
NR_DEV = 8
CAP = 12
NB = 96
NL = 32
NR = 32
N_BOND = 4


def place_ends(values, rng, least, largest):
    dims = values.shape
    place = [jax.random.randint(jax.random.fold_in(rng, axis), (), 0, dims[axis]) for axis in range(len(dims))]
    values = values.at[tuple(place)].set(least)
    longest = dims.index(max(dims))
    place[longest] = (place[longest] + 1) % dims[longest]
    return values.at[tuple(place)].set(largest)


def level_of(rng, extent, cuts, low, largest):
    factor_of = 1.0
    for position, blocks in cuts:
        steps = jax.random.uniform(jax.random.fold_in(jax.random.fold_in(rng, 6), position), (blocks,), jnp.float32, low / len(cuts), largest / len(cuts))
        factor_of = factor_of * jnp.repeat(jnp.exp(steps), extent[position] // blocks).reshape((-1,) + (1,) * (len(extent) - 1 - position))
    return factor_of


def shared_out(stream_key, own, number, rows, number_of, top, most, slope):
    sequence = jax.random.permutation(stream_key, number_of)
    heavy_load, ordinary = portions_of(number_of, rows * top, most, slope, True), portions_of(number_of, rows * top, most, slope, False)
    places = jnp.arange(number_of)

    def named(lengths, turn):
        used = int((lengths > 0).sum())
        fixed = max(1, used // 4)
        shifted = fixed + (places - fixed + turn * (used - fixed)) % max(1, number_of - fixed)
        return jnp.zeros((number_of,), jnp.int32).at[sequence[jnp.where(places < fixed, places, shifted)]].set(jnp.asarray(lengths, jnp.int32))

    lengths = jnp.where(number % 4 == 0, named(heavy_load, number // 4), named(ordinary, number - number // 4 - 1))
    mixed = jax.random.permutation(jax.random.fold_in(own, 3), number_of)
    source_of, receiver = mixed[0:number_of // 2 * 2:2], mixed[1:number_of // 2 * 2:2]
    room = jnp.minimum(lengths[source_of] - 1, most - lengths[receiver]) // 2
    room = jnp.where((source_of == sequence[0]) | (receiver == sequence[0]) | (lengths[receiver] == 0), 0, jnp.maximum(room, 0))
    shifted = jax.random.randint(jax.random.fold_in(own, 4), (number_of // 2,), 0, 1 << 20) % (room + 1)
    lengths = lengths.at[source_of].add(-shifted).at[receiver].add(shifted)
    members = jnp.searchsorted(jnp.cumsum(lengths), jnp.arange(rows * top), side="right").astype(jnp.int32)
    grid = members.reshape(top, rows).T
    grid = grid[jax.random.permutation(jax.random.fold_in(own, 1), rows)]
    turn = jax.random.randint(jax.random.fold_in(own, 2), (rows, 1), 0, top)
    return jnp.take_along_axis(grid, (jnp.arange(top)[None, :] + turn) % top, axis=1)


def portions_of(amount, total, limit, lean, full):
    loads = [(1 << 20) // math.isqrt(standing ** lean) + 1 for standing in range(1, amount + 1)]
    largest = limit if full else min(limit, max(-(-total // amount), total * loads[0] // sum(loads)))
    least = 1 if total - largest >= amount - 1 else 0
    counts, spare = [largest] + [least] * (amount - 1), total - largest - least * (amount - 1)
    while spare > 0:
        candidates = [i for i in range(1, amount) if counts[i] < largest] or [i for i in range(1, amount) if counts[i] < limit]
        mass, budget = sum([loads[i] for i in candidates]), spare
        for i in candidates:
            addition = min(limit - counts[i], max(1, budget * loads[i] // mass), spare)
            counts[i] = counts[i] + addition
            spare = spare - addition
    return np.array(counts)


def scatter_about(rng, extent, spread, most, split=(), kind=jnp.bfloat16):
    values = spread * jax.random.normal(rng, extent, jnp.float32)
    if split:
        values = values * level_of(rng, extent, split, -0.22, 0.18)
    return jnp.clip(values, -most, most).astype(kind)


def setup_inputs(seed: int = 0, part: int = 0) -> dict:
    seeds = jax.random.split(jax.random.key(seed), 10)
    part_keys = jax.random.split(jax.random.fold_in(seeds[9], part), 10)
    psi = scatter_about(part_keys[0], (2, NB, S, S), 1.0, 6.0, ((1, 4), (2, 2)))
    left_env = scatter_about(part_keys[1], (W, NL, S, S), (S * W) ** -0.5, 0.078125, ((0, 2), (1, 4)))
    right_env = scatter_about(part_keys[2], (W, NR, S, S), S ** -0.5, 0.5, ((0, 2), (1, 4), (2, 2)))
    left_sector = place_ends(jax.random.randint(part_keys[3], (NB,), 0, NL_DEV), jax.random.fold_in(part_keys[3], 1), 0, NL_DEV - 1).astype(jnp.int32)
    right_sector = place_ends(jax.random.randint(part_keys[4], (NB,), 0, NR_DEV), jax.random.fold_in(part_keys[4], 1), 0, NR_DEV - 1).astype(jnp.int32)
    dest_device_keys = jax.random.split(jax.random.fold_in(part_keys[5], 1), NB // NB_DEV)
    dest_device_turns = jax.random.permutation(jax.random.fold_in(part_keys[5], 3), NB // NB_DEV)
    dest_device = jax.vmap(lambda own, number: shared_out(jax.random.fold_in(part_keys[5], 2), own, number, NB_DEV, N_BOND, 1, CAP, 2))(dest_device_keys, dest_device_turns).reshape((NB, 1))
    target_block = place_ends(jax.random.randint(part_keys[6], (NB,), 0, NB_DEV), jax.random.fold_in(part_keys[6], 1), 0, NB_DEV - 1).astype(jnp.int32)
    left_size = place_ends(jax.random.randint(part_keys[7], (NL,), 1, S + 1), jax.random.fold_in(part_keys[7], 1), 1, S).astype(jnp.int32)
    right_size = place_ends(jax.random.randint(part_keys[8], (NR,), 1, S + 1), jax.random.fold_in(part_keys[8], 1), 1, S).astype(jnp.int32)
    return dict(psi=psi, left_env=left_env, right_env=right_env, left_sector=left_sector, right_sector=right_sector, dest_device=dest_device, target_block=target_block, left_size=left_size, right_size=right_size)


def mask_blocks(env, sizes):
    states = jnp.arange(env.shape[2], dtype=jnp.int32)
    inside = states[None, :] < sizes[:, None]
    keep = inside[None, :, :, None] & inside[None, :, None, :]
    return jnp.where(keep, env, jnp.zeros_like(env))


def reference(psi, left_env, right_env, left_sector, right_sector, dest_device, target_block, left_size, right_size):
    masked_left = mask_blocks(left_env, left_size)
    masked_right = mask_blocks(right_env, right_size)
    blocks = jnp.arange(NB, dtype=jnp.int32)
    source = blocks // NB_DEV
    left_global = (source * NL_DEV + left_sector).astype(jnp.int32)
    destination = dest_device[:, 0]
    right_global = (destination * NR_DEV + right_sector).astype(jnp.int32)
    target_global = (destination * NB_DEV + target_block).astype(jnp.int32)

    def one_block(index):
        left_piece = masked_left[:, left_global[index]].astype(jnp.float32)
        vector = psi[:, index].astype(jnp.float32)
        half = jnp.einsum('vcb,wab->vwca', vector, left_piece).astype(jnp.bfloat16)
        right_piece = masked_right[:, right_global[index]].astype(jnp.float32)
        return jnp.einsum('vwca,wcd->vad', half.astype(jnp.float32), right_piece)

    results = lax.map(one_block, blocks)
    total = jnp.zeros((2, NB, S, S), jnp.float32)
    total = total.at[:, target_global].add(jnp.transpose(results, (1, 0, 2, 3)))
    return total.astype(jnp.bfloat16)
```

```python
import functools

import jax
import jax.numpy as jnp
from jax import lax
from jax.experimental import pallas as pl
from jax.experimental.pallas import tpu as pltpu
from jax.sharding import PartitionSpec as P

MESH = pl.DeviceIdType.MESH
MIB = 1024 * 1024


def contract_kernel(
    peers,
    steps,
    cap,
    lsec,
    dest,
    rsec,
    lsize,
    rsize,
    slot_src,
    labels,
    psi_hbm,
    left_hbm,
    right_hbm,
    landed,
    lab_out,
    psi_v,
    left_v,
    acc,
    send_a,
    recv_a,
    send_b,
    recv_b,
    mine,
    done,
    send_c,
    chunks,
    psi_sem,
    left_sem,
    own_sem,
    swap_sem,
    lab_send,
    lab_recv,
    lab_own,
    right_send,
    left_send,
    hop_recv,
    a_sem,
    b_sem,
    c_send,
    c_recv,
    c_own,
):
    me = lax.axis_index("bond")
    m = lax.axis_index("mpo")
    s = lax.axis_index("sub")
    other = {"sub": 1 - s}
    half_w = left_v.shape[0]
    wide = half_w // steps
    width = right_hbm.shape[2]
    states = right_hbm.shape[3]
    sectors = right_hbm.shape[1]
    blocks = psi_v.shape[1]
    rows = states // 4

    def remote(src, dst, send_sem, recv_sem, where):
        return pltpu.make_async_remote_copy(
            src_ref=src,
            dst_ref=dst,
            send_sem=send_sem,
            recv_sem=recv_sem,
            device_id=where,
            device_id_type=MESH,
        )

    left_copy = pltpu.make_async_copy(left_hbm.at[pl.ds(s * half_w, half_w)], left_v, left_sem)
    left_copy.start()
    own = []
    for i in range(steps):
        cp = pltpu.make_async_copy(
            right_hbm.at[pl.ds(s * half_w + i * wide, wide)],
            chunks[i].at[me, :, :, pl.ds(s * width, width)],
            own_sem.at[i],
        )
        cp.start()
        own.append(cp)
    psi_own = pltpu.make_async_copy(psi_hbm, psi_v.at[:, :, pl.ds(s * width, width)], psi_sem.at[0])
    psi_own.start()

    barrier = pltpu.get_barrier_semaphore()
    pl.semaphore_signal(barrier, inc=1, device_id=other, device_id_type=MESH)
    pl.semaphore_signal(barrier, inc=1, device_id={"mpo": 1 - m}, device_id_type=MESH)
    for delta in range(1, peers):
        pl.semaphore_signal(
            barrier, inc=1, device_id={"bond": lax.rem(me + delta, peers)}, device_id_type=MESH
        )
    pl.semaphore_wait(barrier, peers + 1)

    swaps = []
    for i in range(steps):
        cp = remote(
            right_hbm.at[pl.ds((1 - s) * half_w + i * wide, wide)],
            chunks[i].at[me, :, :, pl.ds(s * width, width)],
            swap_sem.at[0, i],
            swap_sem.at[1, i],
            other,
        )
        cp.start()
        swaps.append(cp)
    psi_swap = remote(
        psi_hbm, psi_v.at[:, :, pl.ds(s * width, width)], psi_sem.at[1], psi_sem.at[2], other
    )
    psi_swap.start()

    lane = lax.broadcasted_iota(jnp.int32, (states, states), 1)
    row = lax.broadcasted_iota(jnp.int32, (states, states), 0)

    def to_right(i, src):
        return remote(
            chunks[i].at[src],
            chunks[i].at[src],
            right_send.at[i, src],
            hop_recv.at[i, src],
            {"bond": lax.rem(me + 1, peers)},
        )

    def to_left(i, src):
        return remote(
            chunks[i].at[src],
            chunks[i].at[src],
            left_send.at[i, src],
            hop_recv.at[i, src],
            {"bond": lax.rem(me + peers - 1, peers)},
        )

    for i in range(steps):
        own[i].wait()
        swaps[i].wait_recv()

        @pl.loop(0, sectors)
        def _(r):
            keep = jnp.where((lane < rsize[r]) & (row < rsize[r]), 1.0, 0.0).astype(jnp.bfloat16)
            for w in range(wide):
                chunks[i][me, w, r] = chunks[i][me, w, r] * keep

        @pl.when(me < peers - 1)
        def _():
            to_right(i, me).start()

        @pl.when(me > 0)
        def _():
            to_left(i, me).start()

    lab_copies = []
    for delta in range(1, peers):
        q = lax.rem(me + delta, peers)
        cp = remote(labels.at[q], lab_out.at[me], lab_send.at[q], lab_recv.at[me], {"bond": q})
        cp.start()
        lab_copies.append(cp)
    lab_mine = pltpu.make_async_copy(labels.at[me], lab_out.at[me], lab_own)
    lab_mine.start()

    psi_own.wait()
    psi_swap.wait()
    left_copy.wait()

    def forward(h, i):
        @pl.when(me - h >= 0)
        def _():
            to_right(i, me - h).wait_recv()

            @pl.when(me < peers - 1)
            def _():
                to_right(i, me - h).start()

        @pl.when(me + h <= peers - 1)
        def _():
            to_left(i, me + h).wait_recv()

            @pl.when(me > 0)
            def _():
                to_left(i, me + h).start()

    def compute(i):
        @pl.loop(0, blocks)
        def _(k):
            l = lsec[k]
            q = dest[k]
            r = rsec[k]
            keep = jnp.where(lane < lsize[l], 1.0, 0.0).astype(jnp.bfloat16)
            vec = jnp.concatenate([psi_v[0, k] * keep, psi_v[1, k] * keep], axis=0)
            tops, bottoms, pieces = [], [], []
            for w in range(wide):
                out = lax.dot_general(
                    left_v[i * wide + w, l],
                    vec,
                    (((1,), (1,)), ((), ())),
                    preferred_element_type=jnp.float32,
                ).astype(jnp.bfloat16)
                tops.append(out[:, :states])
                bottoms.append(out[:, states:])
                pieces.append(chunks[i][q, w, r])
            lhs = jnp.concatenate(
                [jnp.concatenate(tops, axis=1), jnp.concatenate(bottoms, axis=1)], axis=0
            )
            rhs = jnp.concatenate(pieces, axis=0)
            total = jnp.dot(lhs, rhs, preferred_element_type=jnp.float32)
            if i == 0:
                acc[k] = total
            else:
                acc[k] += total

    for h in range(1, peers - 1):
        for i in range(steps):
            forward(h, i)
    for i in range(steps):
        forward(peers - 1, i)
        compute(i)

    piece_row = lax.broadcasted_iota(jnp.int32, (rows, states), 0)

    def piece(k, v, mm, ss):
        start = mm * (2 * rows) + ss * rows
        value = acc[k, pl.ds(pl.multiple_of(v * states + start, rows), rows)]
        return jnp.where(piece_row + start < lsize[lsec[k]], value, 0.0)

    @pl.loop(0, blocks)
    def _(k):
        for v in range(2):
            for mm in range(2):
                send_a[k, v, mm] = piece(k, v, mm, 1 - s).astype(jnp.bfloat16)

    copy_a = remote(send_a, recv_a, a_sem.at[0], a_sem.at[1], other)
    copy_a.start()
    copy_a.wait()

    @pl.loop(0, blocks)
    def _(k):
        for v in range(2):
            send_b[k, v] = (
                piece(k, v, 1 - m, s) + recv_a[k, v, 1 - m].astype(jnp.float32)
            ).astype(jnp.bfloat16)

    copy_b = remote(send_b, recv_b, b_sem.at[0], b_sem.at[1], {"mpo": 1 - m})
    copy_b.start()

    @pl.loop(0, blocks)
    def _(k):
        for v in range(2):
            mine[k, v] = piece(k, v, m, s) + recv_a[k, v, m].astype(jnp.float32)

    copy_b.wait()

    @pl.loop(0, blocks)
    def _(k):
        for v in range(2):
            done[k, v] = (mine[k, v] + recv_b[k, v].astype(jnp.float32)).astype(jnp.bfloat16)

    c_copies = []
    for delta in range(1, peers + 1):
        q = lax.rem(me + delta, peers)

        @pl.loop(0, cap)
        def _(j):
            send_c[q, j] = done[slot_src[q * cap + j]]

        if delta < peers:
            cp = remote(send_c.at[q], landed.at[me], c_send.at[q], c_recv.at[me], {"bond": q})
        else:
            cp = pltpu.make_async_copy(send_c.at[me], landed.at[me], c_own)
        cp.start()
        c_copies.append(cp)

    for delta in range(1, peers):
        c_copies[delta - 1].wait_send()
        src = lax.rem(me + peers - delta, peers)
        remote(
            send_c.at[src], landed.at[src], c_send.at[src], c_recv.at[src], {"bond": src}
        ).wait_recv()
        lab_copies[delta - 1].wait_send()
        remote(
            labels.at[src], lab_out.at[src], lab_send.at[src], lab_recv.at[src], {"bond": src}
        ).wait_recv()
    c_copies[-1].wait()
    lab_mine.wait()
    for i in range(steps):
        swaps[i].wait_send()
        for h in range(peers):

            @pl.when((me - h >= 0) & (me < peers - 1))
            def _():
                to_right(i, me - h).wait_send()

            @pl.when((me + h <= peers - 1) & (me > 0))
            def _():
                to_left(i, me + h).wait_send()


def add_kernel(peers, cap, labels, landed, out, total):
    total[...] = jnp.zeros_like(total)
    for p in range(peers):

        @pl.loop(0, cap)
        def _(j):
            t = labels[p, 0, j]

            @pl.when(t >= 0)
            def _():
                total[t] += landed[p, j].astype(jnp.float32)

    for v in range(2):
        out[v] = total[:, v].astype(out.dtype)


def body(
    psi,
    left_env,
    right_env,
    left_sector,
    right_sector,
    dest_device,
    target_block,
    left_size,
    right_size,
):
    blocks = psi.shape[1]
    width = psi.shape[2]
    states = psi.shape[3]
    sectors = right_env.shape[1]
    half_w = right_env.shape[0] // 2
    peers = lax.axis_size("bond")
    cap = max(2, 2 * blocks // peers)
    steps = 5
    wide = half_w // steps
    rows = states // 4
    destination = dest_device[:, 0]
    hits = destination[:, None] == jnp.arange(peers, dtype=jnp.int32)[None, :]
    before = jnp.arange(blocks)[None, :] < jnp.arange(blocks)[:, None]
    same = destination[None, :] == destination[:, None]
    rank = jnp.sum((before & same).astype(jnp.int32), axis=1)
    at = hits[:, :, None] & (rank[:, None, None] == jnp.arange(128, dtype=jnp.int32)[None, None, :])
    ids = jnp.arange(blocks, dtype=jnp.int32)
    slot_src = jnp.sum(jnp.where(at, ids[:, None, None], 0), axis=0)[:, :cap].reshape(-1)
    lab = jnp.sum(jnp.where(at, target_block[:, None, None] + 1, 0), axis=0) - 1
    labels = jnp.broadcast_to(lab[:, None, :], (peers, 8, 128)).astype(jnp.int32)

    smem = pl.BlockSpec(memory_space=pltpu.SMEM)
    vmem = pl.BlockSpec(memory_space=pltpu.VMEM)
    hbm = pl.BlockSpec(memory_space=pl.ANY)
    bf16, f32 = jnp.bfloat16, jnp.float32
    dma = pltpu.SemaphoreType.DMA
    landed, lab_in = pl.pallas_call(
        functools.partial(contract_kernel, peers, steps, cap),
        out_shape=(
            jax.ShapeDtypeStruct((peers, cap, 2, rows, states), bf16),
            jax.ShapeDtypeStruct((peers, 8, 128), jnp.int32),
        ),
        in_specs=[smem] * 6 + [vmem] + [hbm] * 3,
        out_specs=(hbm, hbm),
        scratch_shapes=[
            pltpu.VMEM((2, blocks, states, states), bf16),
            pltpu.VMEM((half_w, sectors, states, states), bf16),
            pltpu.VMEM((blocks, 2 * states, states), f32),
            pltpu.VMEM((blocks, 2, 2, rows, states), bf16),
            pltpu.VMEM((blocks, 2, 2, rows, states), bf16),
            pltpu.VMEM((blocks, 2, rows, states), bf16),
            pltpu.VMEM((blocks, 2, rows, states), bf16),
            pltpu.VMEM((blocks, 2, rows, states), f32),
            pltpu.VMEM((blocks, 2, rows, states), bf16),
            pltpu.VMEM((peers, cap, 2, rows, states), bf16),
            [pltpu.VMEM((peers, wide, sectors, states, states), bf16) for _ in range(steps)],
            dma((3,)),
            dma,
            dma((steps,)),
            dma((2, steps)),
            dma((peers,)),
            dma((peers,)),
            dma,
            dma((steps, peers)),
            dma((steps, peers)),
            dma((steps, peers)),
            dma((2,)),
            dma((2,)),
            dma((peers,)),
            dma((peers,)),
            dma,
        ],
        compiler_params=pltpu.CompilerParams(
            collective_id=0, has_side_effects=True, vmem_limit_bytes=60 * MIB
        ),
        name="gather_contract",
    )(
        left_sector,
        destination,
        right_sector,
        left_size,
        right_size,
        slot_src,
        labels,
        psi,
        left_env,
        right_env,
    )
    return pl.pallas_call(
        functools.partial(add_kernel, peers, cap),
        out_shape=jax.ShapeDtypeStruct((2, blocks, rows, states), bf16),
        in_specs=[smem, vmem],
        out_specs=vmem,
        scratch_shapes=[pltpu.VMEM((blocks, 2, rows, states), f32)],
        compiler_params=pltpu.CompilerParams(vmem_limit_bytes=32 * MIB),
        name="add_targets",
    )(lab_in, landed)


def plain_body(
    psi,
    left_env,
    right_env,
    left_sector,
    right_sector,
    dest_device,
    target_block,
    left_size,
    right_size,
):
    blocks = psi.shape[1]
    width = psi.shape[2]
    states = psi.shape[3]
    peers = lax.axis_size("bond")
    capacity = max(2, 2 * blocks // peers)
    slots = peers * capacity
    rows_all = jnp.arange(states, dtype=jnp.int32)
    left_in = rows_all[None, :] < left_size[:, None]
    masked_left = jnp.where(
        left_in[None, :, :, None] & left_in[None, :, None, :], left_env, jnp.zeros_like(left_env)
    )
    col_rows = lax.axis_index("sub") * width + jnp.arange(width, dtype=jnp.int32)
    right_rows = col_rows[None, :] < right_size[:, None]
    right_cols = rows_all[None, :] < right_size[:, None]
    masked_right = jnp.where(
        right_rows[None, :, :, None] & right_cols[None, :, None, :],
        right_env,
        jnp.zeros_like(right_env),
    )
    left_pieces = masked_left[:, left_sector]
    destination = dest_device[:, 0]
    peer_hits = (destination[:, None] == jnp.arange(peers, dtype=jnp.int32)[None, :]).astype(
        jnp.int32
    )
    earlier = jnp.sum(peer_hits * (jnp.cumsum(peer_hits, axis=0) - peer_hits), axis=1)
    slot_of = destination * capacity + earlier
    block_ids = jnp.arange(blocks, dtype=jnp.int32)
    labels = (
        jnp.zeros((slots, 2), jnp.int32)
        .at[slot_of]
        .set(jnp.stack([target_block, right_sector], axis=1))
    )
    half = jnp.einsum(
        "vkcb,wkab->kvwca", psi, left_pieces, preferred_element_type=jnp.float32
    ).astype(jnp.bfloat16)
    empty = jnp.zeros((slots,) + half.shape[1:], jnp.bfloat16)
    received = lax.all_to_all(
        empty.at[slot_of].set(half), "bond", split_axis=0, concat_axis=0, tiled=True
    )
    labels_in = lax.all_to_all(labels, "bond", split_axis=0, concat_axis=0, tiled=True)
    right_pieces = masked_right[:, labels_in[:, 1]]
    product = jnp.einsum(
        "jvwca,wjcd->vjad", received, right_pieces, preferred_element_type=jnp.float32
    )
    placing = (labels_in[:, 0][:, None] == block_ids[None, :]).astype(jnp.float32)
    partial_sum = jnp.einsum("jt,vjad->vtad", placing, product, precision=lax.Precision.HIGHEST)
    return lax.psum_scatter(partial_sum, ("mpo", "sub"), scatter_dimension=2, tiled=True).astype(
        jnp.bfloat16
    )


def solution(mesh):
    in_specs = (
        P(None, ("grp", "bond"), "sub", None),
        P("mpo", ("grp", "bond"), None, None),
        P("mpo", ("grp", "bond"), "sub", None),
        P(("grp", "bond")),
        P(("grp", "bond")),
        P(("grp", "bond"), None),
        P(("grp", "bond")),
        P(("grp", "bond")),
        P(("grp", "bond")),
    )
    out_specs = P(None, ("grp", "bond"), ("mpo", "sub"), None)
    paired = mesh.shape["mpo"] == 2 and mesh.shape["sub"] == 2
    return jax.shard_map(body if paired else plain_body, mesh=mesh, in_specs=in_specs, out_specs=out_specs, check_vma=False)
```

```python
import functools

import jax
import jax.numpy as jnp
from jax import lax
from jax.experimental import pallas as pl
from jax.experimental.pallas import tpu as pltpu
from jax.sharding import PartitionSpec as P

MESH = pl.DeviceIdType.MESH
MIB = 1024 * 1024
UNROLL = 2
LEVELS = (20, 23, 26)


def contract_kernel(
    peers,
    steps,
    cap,
    groups,
    lsec,
    dest,
    offset,
    lsize,
    rsize,
    order,
    order_size,
    slot_src,
    labels,
    psi_hbm,
    left_hbm,
    right_hbm,
    landed,
    lab_out,
    psi_v,
    left_v,
    acc,
    send_a,
    recv_a,
    send_b,
    recv_b,
    mine,
    done,
    send_c,
    stage,
    chunks,
    psi_sem,
    left_sem,
    own_sem,
    swap_sem,
    lab_send,
    lab_recv,
    lab_own,
    right_send,
    left_send,
    hop_recv,
    a_sem,
    b_sem,
    c_send,
    c_recv,
    c_own,
):
    me = lax.axis_index("bond")
    m = lax.axis_index("mpo")
    s = lax.axis_index("sub")
    other = {"sub": 1 - s}
    half_w = left_v.shape[0]
    wide = half_w // steps
    width = psi_hbm.shape[2]
    states = psi_hbm.shape[3]
    parts = right_hbm.shape[2]
    spare = chunks[0].shape[2] - groups
    blocks = psi_v.shape[1]
    rows = states // 4

    def remote(src, dst, send_sem, recv_sem, where):
        return pltpu.make_async_remote_copy(
            src_ref=src,
            dst_ref=dst,
            send_sem=send_sem,
            recv_sem=recv_sem,
            device_id=where,
            device_id_type=MESH,
        )

    left_copy = pltpu.make_async_copy(left_hbm.at[pl.ds(s * half_w, half_w)], left_v, left_sem)
    left_copy.start()
    own = []
    for i in range(steps):
        cp = pltpu.make_async_copy(
            right_hbm.at[pl.ds(s * half_w + i * wide, wide)],
            stage[i].at[:, :, pl.ds(s * parts, parts)],
            own_sem.at[i],
        )
        cp.start()
        own.append(cp)
    psi_own = pltpu.make_async_copy(psi_hbm, psi_v.at[:, :, pl.ds(s * width, width)], psi_sem.at[0])
    psi_own.start()

    barrier = pltpu.get_barrier_semaphore()
    pl.semaphore_signal(barrier, inc=1, device_id=other, device_id_type=MESH)
    pl.semaphore_signal(barrier, inc=1, device_id={"mpo": 1 - m}, device_id_type=MESH)
    for delta in range(1, peers):
        pl.semaphore_signal(
            barrier, inc=1, device_id={"bond": lax.rem(me + delta, peers)}, device_id_type=MESH
        )
    pl.semaphore_wait(barrier, peers + 1)

    swaps = []
    for i in range(steps):
        cp = remote(
            right_hbm.at[pl.ds((1 - s) * half_w + i * wide, wide)],
            stage[i].at[:, :, pl.ds(s * parts, parts)],
            swap_sem.at[0, i],
            swap_sem.at[1, i],
            other,
        )
        cp.start()
        swaps.append(cp)
    psi_swap = remote(
        psi_hbm, psi_v.at[:, :, pl.ds(s * width, width)], psi_sem.at[1], psi_sem.at[2], other
    )
    psi_swap.start()

    lane = lax.broadcasted_iota(jnp.int32, (states, states), 1)
    row = lax.broadcasted_iota(jnp.int32, (states, states), 0)

    def to_right(i, src):
        return remote(
            chunks[i].at[src, :, pl.ds(0, groups)],
            chunks[i].at[src, :, pl.ds(0, groups)],
            right_send.at[i, src],
            hop_recv.at[i, src],
            {"bond": lax.rem(me + 1, peers)},
        )

    def to_left(i, src):
        return remote(
            chunks[i].at[src, :, pl.ds(0, groups)],
            chunks[i].at[src, :, pl.ds(0, groups)],
            left_send.at[i, src],
            hop_recv.at[i, src],
            {"bond": lax.rem(me + peers - 1, peers)},
        )

    for i in range(steps):
        own[i].wait()
        swaps[i].wait_recv()

        @pl.loop(0, groups, unroll=4)
        def _(g):
            keep = jnp.where(lane[:16] < order_size[g], 1.0, 0.0).astype(jnp.bfloat16)
            r = order[g] // (2 * parts)
            part = order[g] % (2 * parts)
            for w in range(wide):
                chunks[i][me, w, g] = stage[i][w, r, part] * keep

        @pl.when(me < peers - 1)
        def _():
            to_right(i, me).start()

        @pl.when(me > 0)
        def _():
            to_left(i, me).start()

    lab_copies = []
    for delta in range(1, peers):
        q = lax.rem(me + delta, peers)
        cp = remote(labels.at[q], lab_out.at[me], lab_send.at[q], lab_recv.at[me], {"bond": q})
        cp.start()
        lab_copies.append(cp)
    lab_mine = pltpu.make_async_copy(labels.at[me], lab_out.at[me], lab_own)
    lab_mine.start()

    for i in range(steps):
        for p in range(peers):
            chunks[i][p, :, groups:] = jnp.zeros((wide, spare) + chunks[i].shape[3:], jnp.bfloat16)

    psi_own.wait()
    psi_swap.wait()
    left_copy.wait()

    def forward(h, i):
        @pl.when(me - h >= 0)
        def _():
            to_right(i, me - h).wait_recv()

            @pl.when(me < peers - 1)
            def _():
                to_right(i, me - h).start()

        @pl.when(me + h <= peers - 1)
        def _():
            to_left(i, me + h).wait_recv()

            @pl.when(me > 0)
            def _():
                to_left(i, me + h).start()

    def compute(i):
        @pl.loop(0, blocks, unroll=UNROLL)
        def _(k):
            l = lsec[k]
            q = dest[k]
            start = offset[k]
            inside = (lane < lsize[l]) & (row < rsize[k])
            keep = jnp.where(inside, 1.0, 0.0).astype(jnp.bfloat16)
            vec = jnp.concatenate([psi_v[0, k] * keep, psi_v[1, k] * keep], axis=0)
            tops, bottoms, pieces = [], [], []
            for w in range(wide):
                out = lax.dot_general(
                    left_v[i * wide + w, l],
                    vec,
                    (((1,), (1,)), ((), ())),
                    preferred_element_type=jnp.float32,
                ).astype(jnp.bfloat16)
                tops.append(out[:, :states])
                bottoms.append(out[:, states:])
                pieces.append(
                    chunks[i][q, w, pl.ds(start, 2 * parts)].reshape(states, states)
                )
            lhs = jnp.concatenate(
                [jnp.concatenate(tops, axis=1), jnp.concatenate(bottoms, axis=1)], axis=0
            )
            rhs = jnp.concatenate(pieces, axis=0)
            total = jnp.dot(lhs, rhs, preferred_element_type=jnp.float32)
            if i == 0:
                acc[k] = total
            else:
                acc[k] += total

    for h in range(1, peers - 1):
        for i in range(steps):
            forward(h, i)
    for i in range(steps):
        forward(peers - 1, i)
        compute(i)

    piece_row = lax.broadcasted_iota(jnp.int32, (rows, states), 0)

    def piece(k, v, mm, ss):
        start = mm * (2 * rows) + ss * rows
        value = acc[k, pl.ds(pl.multiple_of(v * states + start, rows), rows)]
        return jnp.where(piece_row + start < lsize[lsec[k]], value, 0.0)

    @pl.loop(0, blocks)
    def _(k):
        for v in range(2):
            for mm in range(2):
                send_a[k, v, mm] = piece(k, v, mm, 1 - s).astype(jnp.bfloat16)

    copy_a = remote(send_a, recv_a, a_sem.at[0], a_sem.at[1], other)
    copy_a.start()
    copy_a.wait()

    @pl.loop(0, blocks)
    def _(k):
        for v in range(2):
            send_b[k, v] = (
                piece(k, v, 1 - m, s) + recv_a[k, v, 1 - m].astype(jnp.float32)
            ).astype(jnp.bfloat16)

    copy_b = remote(send_b, recv_b, b_sem.at[0], b_sem.at[1], {"mpo": 1 - m})
    copy_b.start()

    @pl.loop(0, blocks)
    def _(k):
        for v in range(2):
            mine[k, v] = piece(k, v, m, s) + recv_a[k, v, m].astype(jnp.float32)

    copy_b.wait()

    @pl.loop(0, blocks)
    def _(k):
        for v in range(2):
            done[k, v] = (mine[k, v] + recv_b[k, v].astype(jnp.float32)).astype(jnp.bfloat16)

    c_copies = []
    for delta in range(1, peers + 1):
        q = lax.rem(me + delta, peers)

        @pl.loop(0, cap)
        def _(j):
            send_c[q, j] = done[slot_src[q * cap + j]]

        if delta < peers:
            cp = remote(send_c.at[q], landed.at[me], c_send.at[q], c_recv.at[me], {"bond": q})
        else:
            cp = pltpu.make_async_copy(send_c.at[me], landed.at[me], c_own)
        cp.start()
        c_copies.append(cp)

    for delta in range(1, peers):
        c_copies[delta - 1].wait_send()
        src = lax.rem(me + peers - delta, peers)
        remote(
            send_c.at[src], landed.at[src], c_send.at[src], c_recv.at[src], {"bond": src}
        ).wait_recv()
        lab_copies[delta - 1].wait_send()
        remote(
            labels.at[src], lab_out.at[src], lab_send.at[src], lab_recv.at[src], {"bond": src}
        ).wait_recv()
    c_copies[-1].wait()
    lab_mine.wait()
    for i in range(steps):
        swaps[i].wait_send()
        for h in range(peers):

            @pl.when((me - h >= 0) & (me < peers - 1))
            def _():
                to_right(i, me - h).wait_send()

            @pl.when((me + h <= peers - 1) & (me > 0))
            def _():
                to_left(i, me + h).wait_send()


def add_kernel(peers, cap, labels, landed, out, total):
    total[...] = jnp.zeros_like(total)
    for p in range(peers):

        @pl.loop(0, cap)
        def _(j):
            t = labels[p, 0, j]

            @pl.when(t >= 0)
            def _():
                total[t] += landed[p, j].astype(jnp.float32)

    for v in range(2):
        out[v] = total[:, v].astype(out.dtype)


def body(
    psi,
    left_env,
    right_env,
    left_sector,
    right_sector,
    dest_device,
    target_block,
    left_size,
    right_size,
):
    blocks = psi.shape[1]
    width = psi.shape[2]
    states = psi.shape[3]
    sectors = right_env.shape[1]
    half_w = right_env.shape[0] // 2
    peers = lax.axis_size("bond")
    cap = max(2, 2 * blocks // peers)
    steps = 5
    wide = half_w // steps
    rows = states // 4
    destination = dest_device[:, 0]
    hits = destination[:, None] == jnp.arange(peers, dtype=jnp.int32)[None, :]
    before = jnp.arange(blocks)[None, :] < jnp.arange(blocks)[:, None]
    same = destination[None, :] == destination[:, None]
    rank = jnp.sum((before & same).astype(jnp.int32), axis=1)
    at = hits[:, :, None] & (rank[:, None, None] == jnp.arange(128, dtype=jnp.int32)[None, None, :])
    ids = jnp.arange(blocks, dtype=jnp.int32)
    slot_src = jnp.sum(jnp.where(at, ids[:, None, None], 0), axis=0)[:, :cap].reshape(-1)
    lab = jnp.sum(jnp.where(at, target_block[:, None, None] + 1, 0), axis=0) - 1
    labels = jnp.broadcast_to(lab[:, None, :], (peers, 8, 128)).astype(jnp.int32)

    group = 16
    per = states // group
    total_groups = sectors * per
    sizes = lax.all_gather(right_size, ("grp", "bond"), axis=0, tiled=True).reshape(-1, sectors)
    counts = (sizes + (group - 1)) // group
    need = jnp.max(jnp.sum(counts, axis=1))
    low = jnp.tril(jnp.ones((sectors, sectors), jnp.int32), -1)
    starts = jnp.sum(counts[:, None, :] * low[None], axis=2)
    part = lax.axis_index("grp")
    sizes_here = lax.dynamic_slice_in_dim(sizes, part * peers, peers, 0)
    starts_here = lax.dynamic_slice_in_dim(starts, part * peers, peers, 0)
    named = (destination * sectors + right_sector)[:, None] == jnp.arange(peers * sectors)[None, :]
    offset = jnp.sum(jnp.where(named, starts_here.reshape(1, -1), 0), axis=1)
    rsize = jnp.sum(jnp.where(named, sizes_here.reshape(1, -1), 0), axis=1)
    own_counts = (right_size + (group - 1)) // group
    own_starts = jnp.sum(own_counts[None, :] * low, axis=1)
    each = jnp.arange(total_groups, dtype=jnp.int32).reshape(sectors, per)
    inner = jnp.arange(per, dtype=jnp.int32)[None, :]
    place = jnp.where(inner < own_counts[:, None], own_starts[:, None] + inner, -1)
    fits = place[None] == jnp.arange(total_groups, dtype=jnp.int32)[:, None, None]
    order = jnp.sum(jnp.where(fits, each[None], 0), axis=(1, 2))
    order_size = jnp.sum(jnp.where(fits, right_size[None, :, None], 0), axis=(1, 2))
    levels = [total_groups * f // 32 for f in LEVELS] + [total_groups]
    level = sum((need > at).astype(jnp.int32) for at in levels[:-1])

    smem = pl.BlockSpec(memory_space=pltpu.SMEM)
    vmem = pl.BlockSpec(memory_space=pltpu.VMEM)
    hbm = pl.BlockSpec(memory_space=pl.ANY)
    bf16, f32 = jnp.bfloat16, jnp.float32
    dma = pltpu.SemaphoreType.DMA
    def contract(number, groups, *operands):
        return pl.pallas_call(
            functools.partial(contract_kernel, peers, steps, cap, groups),
            out_shape=(
                jax.ShapeDtypeStruct((peers, cap, 2, rows, states), bf16),
                jax.ShapeDtypeStruct((peers, 8, 128), jnp.int32),
            ),
            in_specs=[smem] * 8 + [vmem] + [hbm] * 3,
            out_specs=(hbm, hbm),
            scratch_shapes=[
                pltpu.VMEM((2, blocks, states, states), bf16),
                pltpu.VMEM((half_w, sectors, states, states), bf16),
                pltpu.VMEM((blocks, 2 * states, states), f32),
                pltpu.VMEM((blocks, 2, 2, rows, states), bf16),
                pltpu.VMEM((blocks, 2, 2, rows, states), bf16),
                pltpu.VMEM((blocks, 2, rows, states), bf16),
                pltpu.VMEM((blocks, 2, rows, states), bf16),
                pltpu.VMEM((blocks, 2, rows, states), f32),
                pltpu.VMEM((blocks, 2, rows, states), bf16),
                pltpu.VMEM((peers, cap, 2, rows, states), bf16),
                [pltpu.VMEM((wide, sectors, per, group, states), bf16) for _ in range(steps)],
                [
                    pltpu.VMEM((peers, wide, groups + per, group, states), bf16)
                    for _ in range(steps)
                ],
                dma((3,)),
                dma,
                dma((steps,)),
                dma((2, steps)),
                dma((peers,)),
                dma((peers,)),
                dma,
                dma((steps, peers)),
                dma((steps, peers)),
                dma((steps, peers)),
                dma((2,)),
                dma((2,)),
                dma((peers,)),
                dma((peers,)),
                dma,
            ],
            compiler_params=pltpu.CompilerParams(
                collective_id=number, has_side_effects=True, vmem_limit_bytes=60 * MIB
            ),
            name="gather_contract_%d" % groups,
        )(*operands)

    landed, lab_in = lax.switch(
        level,
        [functools.partial(contract, i, groups) for i, groups in enumerate(levels)],
        left_sector,
        destination,
        offset,
        left_size,
        rsize,
        order,
        order_size,
        slot_src,
        labels,
        psi,
        left_env,
        right_env.reshape(right_env.shape[:2] + (width // group, group, states)),
    )
    return pl.pallas_call(
        functools.partial(add_kernel, peers, cap),
        out_shape=jax.ShapeDtypeStruct((2, blocks, rows, states), bf16),
        in_specs=[smem, vmem],
        out_specs=vmem,
        scratch_shapes=[pltpu.VMEM((blocks, 2, rows, states), f32)],
        compiler_params=pltpu.CompilerParams(vmem_limit_bytes=32 * MIB),
        name="add_targets",
    )(lab_in, landed)


def plain_body(
    psi,
    left_env,
    right_env,
    left_sector,
    right_sector,
    dest_device,
    target_block,
    left_size,
    right_size,
):
    blocks = psi.shape[1]
    width = psi.shape[2]
    states = psi.shape[3]
    peers = lax.axis_size("bond")
    capacity = max(2, 2 * blocks // peers)
    slots = peers * capacity
    rows_all = jnp.arange(states, dtype=jnp.int32)
    left_in = rows_all[None, :] < left_size[:, None]
    masked_left = jnp.where(
        left_in[None, :, :, None] & left_in[None, :, None, :], left_env, jnp.zeros_like(left_env)
    )
    col_rows = lax.axis_index("sub") * width + jnp.arange(width, dtype=jnp.int32)
    right_rows = col_rows[None, :] < right_size[:, None]
    right_cols = rows_all[None, :] < right_size[:, None]
    masked_right = jnp.where(
        right_rows[None, :, :, None] & right_cols[None, :, None, :],
        right_env,
        jnp.zeros_like(right_env),
    )
    left_pieces = masked_left[:, left_sector]
    destination = dest_device[:, 0]
    peer_hits = (destination[:, None] == jnp.arange(peers, dtype=jnp.int32)[None, :]).astype(
        jnp.int32
    )
    earlier = jnp.sum(peer_hits * (jnp.cumsum(peer_hits, axis=0) - peer_hits), axis=1)
    slot_of = destination * capacity + earlier
    block_ids = jnp.arange(blocks, dtype=jnp.int32)
    labels = (
        jnp.zeros((slots, 2), jnp.int32)
        .at[slot_of]
        .set(jnp.stack([target_block, right_sector], axis=1))
    )
    half = jnp.einsum(
        "vkcb,wkab->kvwca", psi, left_pieces, preferred_element_type=jnp.float32
    ).astype(jnp.bfloat16)
    empty = jnp.zeros((slots,) + half.shape[1:], jnp.bfloat16)
    received = lax.all_to_all(
        empty.at[slot_of].set(half), "bond", split_axis=0, concat_axis=0, tiled=True
    )
    labels_in = lax.all_to_all(labels, "bond", split_axis=0, concat_axis=0, tiled=True)
    right_pieces = masked_right[:, labels_in[:, 1]]
    product = jnp.einsum(
        "jvwca,wjcd->vjad", received, right_pieces, preferred_element_type=jnp.float32
    )
    placing = (labels_in[:, 0][:, None] == block_ids[None, :]).astype(jnp.float32)
    partial_sum = jnp.einsum("jt,vjad->vtad", placing, product, precision=lax.Precision.HIGHEST)
    return lax.psum_scatter(partial_sum, ("mpo", "sub"), scatter_dimension=2, tiled=True).astype(
        jnp.bfloat16
    )


def solution(mesh):
    in_specs = (
        P(None, ("grp", "bond"), "sub", None),
        P("mpo", ("grp", "bond"), None, None),
        P("mpo", ("grp", "bond"), "sub", None),
        P(("grp", "bond")),
        P(("grp", "bond")),
        P(("grp", "bond"), None),
        P(("grp", "bond")),
        P(("grp", "bond")),
        P(("grp", "bond")),
    )
    out_specs = P(None, ("grp", "bond"), ("mpo", "sub"), None)
    paired = mesh.shape["mpo"] == 2 and mesh.shape["sub"] == 2
    return jax.shard_map(body if paired else plain_body, mesh=mesh, in_specs=in_specs, out_specs=out_specs, check_vma=False)
```

```python
import functools

import jax
import jax.numpy as jnp
from jax import lax
from jax.experimental import pallas as pl
from jax.experimental.pallas import tpu as pltpu
from jax.sharding import PartitionSpec as P

MESH = pl.DeviceIdType.MESH
MIB = 1024 * 1024
UNROLL = 2
LEVELS = (17, 18, 19, 20, 21, 22, 23, 24, 25, 27)


def contract_kernel(
    peers,
    steps,
    cap,
    groups,
    lsec,
    dest,
    rsec,
    lsize,
    sizes,
    slots,
    labels,
    psi_hbm,
    left_hbm,
    right_hbm,
    landed,
    lab_out,
    psi_v,
    left_v,
    acc,
    send_a,
    recv_a,
    send_b,
    recv_b,
    mine,
    done,
    send_c,
    stage,
    chunks,
    psi_sem,
    left_sem,
    own_sem,
    swap_sem,
    lab_send,
    lab_recv,
    lab_own,
    right_send,
    left_send,
    hop_recv,
    a_sem,
    b_sem,
    c_send,
    c_recv,
    c_own,
    starts,
    order_sector,
    order_part,
    order_size,
):
    me = lax.axis_index("bond")
    m = lax.axis_index("mpo")
    s = lax.axis_index("sub")
    other = {"sub": 1 - s}
    half_w = left_v.shape[0]
    wide = half_w // steps
    width = psi_hbm.shape[2]
    states = psi_hbm.shape[3]
    parts = right_hbm.shape[2]
    spare = chunks[0].shape[2] - groups
    blocks = psi_v.shape[1]
    rows = states // 4

    def remote(src, dst, send_sem, recv_sem, where):
        return pltpu.make_async_remote_copy(
            src_ref=src,
            dst_ref=dst,
            send_sem=send_sem,
            recv_sem=recv_sem,
            device_id=where,
            device_id_type=MESH,
        )

    left_copy = pltpu.make_async_copy(left_hbm.at[pl.ds(s * half_w, half_w)], left_v, left_sem)
    left_copy.start()
    own = []
    for i in range(steps):
        cp = pltpu.make_async_copy(
            right_hbm.at[pl.ds(s * half_w + i * wide, wide)],
            stage[i].at[:, :, pl.ds(s * parts, parts)],
            own_sem.at[i],
        )
        cp.start()
        own.append(cp)
    psi_own = pltpu.make_async_copy(psi_hbm, psi_v.at[:, :, pl.ds(s * width, width)], psi_sem.at[0])
    psi_own.start()

    barrier = pltpu.get_barrier_semaphore()
    pl.semaphore_signal(barrier, inc=1, device_id=other, device_id_type=MESH)
    pl.semaphore_signal(barrier, inc=1, device_id={"mpo": 1 - m}, device_id_type=MESH)
    for delta in range(1, peers):
        pl.semaphore_signal(
            barrier, inc=1, device_id={"bond": lax.rem(me + delta, peers)}, device_id_type=MESH
        )
    pl.semaphore_wait(barrier, peers + 1)

    swaps = []
    for i in range(steps):
        cp = remote(
            right_hbm.at[pl.ds((1 - s) * half_w + i * wide, wide)],
            stage[i].at[:, :, pl.ds(s * parts, parts)],
            swap_sem.at[0, i],
            swap_sem.at[1, i],
            other,
        )
        cp.start()
        swaps.append(cp)
    psi_swap = remote(
        psi_hbm, psi_v.at[:, :, pl.ds(s * width, width)], psi_sem.at[1], psi_sem.at[2], other
    )
    psi_swap.start()

    sectors = right_hbm.shape[1]
    first = lax.axis_index("grp") * peers
    group = right_hbm.shape[3]

    @pl.loop(0, peers)
    def _(p):
        run = 0
        for r in range(sectors):
            starts[p * sectors + r] = run
            run += (sizes[first + p, 0, r] + (group - 1)) // group

    def next_group(g, carry):
        r, part = carry
        safe = jnp.minimum(r, sectors - 1)
        size = sizes[first + me, 0, safe]
        order_sector[g] = safe
        order_part[g] = part
        order_size[g] = jnp.where(r < sectors, size, 0)
        last = (part + 1) * group >= size
        return jnp.where(last, r + 1, r), jnp.where(last, 0, part + 1)

    lax.fori_loop(0, groups, next_group, (jnp.int32(0), jnp.int32(0)))

    lane = lax.broadcasted_iota(jnp.int32, (states, states), 1)
    row = lax.broadcasted_iota(jnp.int32, (states, states), 0)

    def to_right(i, src):
        return remote(
            chunks[i].at[src, :, pl.ds(0, groups)],
            chunks[i].at[src, :, pl.ds(0, groups)],
            right_send.at[i, src],
            hop_recv.at[i, src],
            {"bond": lax.rem(me + 1, peers)},
        )

    def to_left(i, src):
        return remote(
            chunks[i].at[src, :, pl.ds(0, groups)],
            chunks[i].at[src, :, pl.ds(0, groups)],
            left_send.at[i, src],
            hop_recv.at[i, src],
            {"bond": lax.rem(me + peers - 1, peers)},
        )

    for i in range(steps):
        own[i].wait()
        swaps[i].wait_recv()

        @pl.loop(0, groups, unroll=4)
        def _(g):
            keep = jnp.where(lane[:16] < order_size[g], 1.0, 0.0).astype(jnp.bfloat16)
            r = order_sector[g]
            part = order_part[g]
            for w in range(wide):
                chunks[i][me, w, g] = stage[i][w, r, part] * keep

        @pl.when(me < peers - 1)
        def _():
            to_right(i, me).start()

        @pl.when(me > 0)
        def _():
            to_left(i, me).start()

    lab_copies = []
    for delta in range(1, peers):
        q = lax.rem(me + delta, peers)
        cp = remote(labels.at[q], lab_out.at[me], lab_send.at[q], lab_recv.at[me], {"bond": q})
        cp.start()
        lab_copies.append(cp)
    lab_mine = pltpu.make_async_copy(labels.at[me], lab_out.at[me], lab_own)
    lab_mine.start()

    for i in range(steps):
        for p in range(peers):
            chunks[i][p, :, groups:] = jnp.zeros((wide, spare) + chunks[i].shape[3:], jnp.bfloat16)

    psi_own.wait()
    psi_swap.wait()
    left_copy.wait()

    def forward(h, i):
        @pl.when(me - h >= 0)
        def _():
            to_right(i, me - h).wait_recv()

            @pl.when(me < peers - 1)
            def _():
                to_right(i, me - h).start()

        @pl.when(me + h <= peers - 1)
        def _():
            to_left(i, me + h).wait_recv()

            @pl.when(me > 0)
            def _():
                to_left(i, me + h).start()

    def compute(i):
        @pl.loop(0, blocks, unroll=UNROLL)
        def _(k):
            l = lsec[k]
            q = dest[k]
            r = rsec[k]
            start = starts[q * sectors + r]
            inside = (lane < lsize[l]) & (row < sizes[first + q, 0, r])
            keep = jnp.where(inside, 1.0, 0.0).astype(jnp.bfloat16)
            vec = jnp.concatenate([psi_v[0, k] * keep, psi_v[1, k] * keep], axis=0)
            tops, bottoms, pieces = [], [], []
            for w in range(wide):
                out = lax.dot_general(
                    left_v[i * wide + w, l],
                    vec,
                    (((1,), (1,)), ((), ())),
                    preferred_element_type=jnp.float32,
                ).astype(jnp.bfloat16)
                tops.append(out[:, :states])
                bottoms.append(out[:, states:])
                pieces.append(
                    chunks[i][q, w, pl.ds(start, 2 * parts)].reshape(states, states)
                )
            lhs = jnp.concatenate(
                [jnp.concatenate(tops, axis=1), jnp.concatenate(bottoms, axis=1)], axis=0
            )
            rhs = jnp.concatenate(pieces, axis=0)
            total = jnp.dot(lhs, rhs, preferred_element_type=jnp.float32)
            if i == 0:
                acc[k] = total
            else:
                acc[k] += total

    for h in range(1, peers - 1):
        for i in range(steps):
            forward(h, i)
    for i in range(steps):
        forward(peers - 1, i)
        compute(i)

    piece_row = lax.broadcasted_iota(jnp.int32, (rows, states), 0)

    def piece(k, v, mm, ss):
        start = mm * (2 * rows) + ss * rows
        value = acc[k, pl.ds(pl.multiple_of(v * states + start, rows), rows)]
        return jnp.where(piece_row + start < lsize[lsec[k]], value, 0.0)

    def copy_a(v):
        return remote(send_a.at[v], recv_a.at[v], a_sem.at[0, v], a_sem.at[1, v], other)

    def copy_b(v):
        return remote(send_b.at[v], recv_b.at[v], b_sem.at[0, v], b_sem.at[1, v], {"mpo": 1 - m})

    def copy_c(v, q, src):
        return remote(
            send_c.at[q, v], landed.at[src, v], c_send.at[v, q], c_recv.at[v, src], {"bond": q}
        )

    def own_c(v):
        return pltpu.make_async_copy(send_c.at[me, v], landed.at[me, v], c_own.at[v])

    for v in range(2):

        @pl.loop(0, blocks, unroll=2)
        def _(k):
            for mm in range(2):
                send_a[v, k, mm] = piece(k, v, mm, 1 - s).astype(jnp.bfloat16)

        copy_a(v).start()

    for v in range(2):
        copy_a(v).wait_recv()

        @pl.loop(0, blocks, unroll=2)
        def _(k):
            send_b[v, k] = (
                piece(k, v, 1 - m, s) + recv_a[v, k, 1 - m].astype(jnp.float32)
            ).astype(jnp.bfloat16)

        copy_b(v).start()

    for v in range(2):

        @pl.loop(0, blocks, unroll=2)
        def _(k):
            mine[v, k] = piece(k, v, m, s) + recv_a[v, k, m].astype(jnp.float32)

    for v in range(2):
        copy_b(v).wait_recv()

        @pl.loop(0, blocks, unroll=2)
        def _(k):
            done[v][k] = (mine[v, k] + recv_b[v, k].astype(jnp.float32)).astype(jnp.bfloat16)

        for delta in range(1, peers + 1):
            q = lax.rem(me + delta, peers)

            @pl.loop(0, cap, unroll=2)
            def _(j):
                send_c[q, v, j] = done[v][slots[q, 0, j]]

            if delta < peers:
                copy_c(v, q, me).start()
            else:
                own_c(v).start()

    for v in range(2):
        copy_a(v).wait_send()
        copy_b(v).wait_send()
        own_c(v).wait()
        for delta in range(1, peers):
            q = lax.rem(me + delta, peers)
            copy_c(v, q, me).wait_send()
            copy_c(v, q, q).wait_recv()

    for delta in range(1, peers):
        lab_copies[delta - 1].wait_send()
        src = lax.rem(me + peers - delta, peers)
        remote(
            labels.at[src], lab_out.at[src], lab_send.at[src], lab_recv.at[src], {"bond": src}
        ).wait_recv()
    lab_mine.wait()
    for i in range(steps):
        swaps[i].wait_send()
        for h in range(peers):

            @pl.when((me - h >= 0) & (me < peers - 1))
            def _():
                to_right(i, me - h).wait_send()

            @pl.when((me + h <= peers - 1) & (me > 0))
            def _():
                to_left(i, me + h).wait_send()


def add_kernel(peers, cap, labels, landed, out, total):
    total[...] = jnp.zeros_like(total)
    for p in range(peers):

        @pl.loop(0, cap)
        def _(j):
            t = labels[p, 0, j]

            @pl.when(t >= 0)
            def _():
                for v in range(2):
                    total[v, t] += landed[p, v, j].astype(jnp.float32)

    out[...] = total[...].astype(out.dtype)


def share_kernel(
    peers, group, levels, own, dest_col, dest_row, target_col, sizes, slots, labels, level,
    send_sem, recv_sem, own_sem
):
    g, me = lax.axis_index("grp"), lax.axis_index("bond")
    parts = lax.axis_size("grp")
    mine = g * peers + me
    far = [(a, b) for a in range(parts) for b in range(peers) if a or b]

    def place(a, b):
        return lax.rem(g + a, parts), lax.rem(me + b, peers)

    barrier = pltpu.get_barrier_semaphore()
    for a, b in far:
        x, y = place(a, b)
        pl.semaphore_signal(
            barrier, inc=1, device_id={"grp": x, "bond": y}, device_id_type=MESH
        )
    own_copy = pltpu.make_async_copy(own, sizes.at[mine], own_sem)
    own_copy.start()
    pl.semaphore_wait(barrier, len(far))

    def copy(slot, a, b):
        x, y = place(a, b)
        return pltpu.make_async_remote_copy(
            src_ref=own,
            dst_ref=sizes.at[slot],
            send_sem=send_sem.at[x * peers + y],
            recv_sem=recv_sem.at[slot],
            device_id={"grp": x, "bond": y},
            device_id_type=MESH,
        )

    for a, b in far:
        copy(mine, a, b).start()

    blocks = dest_col.shape[0]
    col, line = dest_col[...], dest_row[...]
    ks = lax.broadcasted_iota(jnp.int32, (blocks, blocks), 0)
    js = lax.broadcasted_iota(jnp.int32, (blocks, blocks), 1)
    rank = jnp.sum(jnp.where((col == line) & (js < ks), 1, 0), axis=1, keepdims=True)
    lane = lax.broadcasted_iota(jnp.int32, (blocks, 128), 1)
    ids = lax.broadcasted_iota(jnp.int32, (blocks, 128), 0)
    named = target_col[...] + 1
    for q in range(peers):
        at = (col == q) & (rank == lane)
        slots[q] = jnp.broadcast_to(
            jnp.sum(jnp.where(at, ids, 0), axis=0, keepdims=True), (8, 128)
        )
        labels[q] = jnp.broadcast_to(
            jnp.sum(jnp.where(at, named, 0), axis=0, keepdims=True) - 1, (8, 128)
        )

    own_copy.wait()
    for a, b in far:
        x, y = place(a, b)
        copy(mine, a, b).wait_send()
        copy(x * peers + y, a, b).wait_recv()
    most = jnp.zeros((8, 1), jnp.int32)
    for p in range(parts * peers):
        count = lax.shift_right_logical(sizes[p] + (group - 1), group.bit_length() - 1)
        most = jnp.maximum(most, jnp.sum(count, axis=1, keepdims=True))
    found = jnp.zeros((8, 1), jnp.int32)
    for edge in levels[:-1]:
        found += jnp.where(most > edge, 1, 0)
    level[...] = jnp.broadcast_to(found, (8, 128))


def body(
    psi,
    left_env,
    right_env,
    left_sector,
    right_sector,
    dest_device,
    target_block,
    left_size,
    right_size,
):
    blocks = psi.shape[1]
    width = psi.shape[2]
    states = psi.shape[3]
    sectors = right_env.shape[1]
    half_w = right_env.shape[0] // 2
    peers = lax.axis_size("bond")
    cap = max(2, 2 * blocks // peers)
    steps = 5
    wide = half_w // steps
    rows = states // 4
    destination = dest_device[:, 0]
    smem = pl.BlockSpec(memory_space=pltpu.SMEM)
    vmem = pl.BlockSpec(memory_space=pltpu.VMEM)
    hbm = pl.BlockSpec(memory_space=pl.ANY)
    bf16, f32, i32 = jnp.bfloat16, jnp.float32, jnp.int32
    dma = pltpu.SemaphoreType.DMA
    group = 16
    per = states // group
    total_groups = sectors * per
    levels = [total_groups * f // 32 for f in LEVELS] + [total_groups]
    owners = lax.axis_size("grp") * peers
    own_sizes = jnp.pad(
        jnp.broadcast_to(right_size[None, :], (8, sectors)), ((0, 0), (0, 128 - sectors))
    )
    sizes, slots, labels, level = pl.pallas_call(
        functools.partial(share_kernel, peers, group, levels),
        out_shape=(
            jax.ShapeDtypeStruct((owners, 8, 128), i32),
            jax.ShapeDtypeStruct((peers, 8, 128), i32),
            jax.ShapeDtypeStruct((peers, 8, 128), i32),
            jax.ShapeDtypeStruct((8, 128), i32),
        ),
        in_specs=[vmem] * 4,
        out_specs=(vmem,) * 4,
        scratch_shapes=[dma((owners,)), dma((owners,)), dma],
        compiler_params=pltpu.CompilerParams(collective_id=0, has_side_effects=True),
        name="share_sizes",
    )(own_sizes, dest_device, destination.reshape(1, -1), target_block.reshape(-1, 1))

    def contract(number, groups, *operands):
        return pl.pallas_call(
            functools.partial(contract_kernel, peers, steps, cap, groups),
            out_shape=(
                jax.ShapeDtypeStruct((peers, 2, cap, rows, states), bf16),
                jax.ShapeDtypeStruct((peers, 8, 128), jnp.int32),
            ),
            in_specs=[smem] * 6 + [vmem] + [hbm] * 3,
            out_specs=(hbm, hbm),
            scratch_shapes=[
                pltpu.VMEM((2, blocks, states, states), bf16),
                pltpu.VMEM((half_w, sectors, states, states), bf16),
                pltpu.VMEM((blocks, 2 * states, states), f32),
                pltpu.VMEM((2, blocks, 2, rows, states), bf16),
                pltpu.VMEM((2, blocks, 2, rows, states), bf16),
                pltpu.VMEM((2, blocks, rows, states), bf16),
                pltpu.VMEM((2, blocks, rows, states), bf16),
                pltpu.VMEM((2, blocks, rows, states), f32),
                [pltpu.VMEM((blocks, rows, states), bf16) for _ in range(2)],
                pltpu.VMEM((peers, 2, cap, rows, states), bf16),
                [pltpu.VMEM((wide, sectors, per, group, states), bf16) for _ in range(steps)],
                [
                    pltpu.VMEM((peers, wide, groups + per, group, states), bf16)
                    for _ in range(steps)
                ],
                dma((3,)),
                dma,
                dma((steps,)),
                dma((2, steps)),
                dma((peers,)),
                dma((peers,)),
                dma,
                dma((steps, peers)),
                dma((steps, peers)),
                dma((steps, peers)),
                dma((2, 2)),
                dma((2, 2)),
                dma((2, peers)),
                dma((2, peers)),
                dma((2,)),
                pltpu.SMEM((peers * sectors,), i32),
                pltpu.SMEM((total_groups,), i32),
                pltpu.SMEM((total_groups,), i32),
                pltpu.SMEM((total_groups,), i32),
            ],
            compiler_params=pltpu.CompilerParams(
                collective_id=number + 1, has_side_effects=True, vmem_limit_bytes=60 * MIB
            ),
            name="gather_contract_%d" % groups,
        )(*operands)

    landed, lab_in = lax.switch(
        level[0, 0],
        [functools.partial(contract, i, groups) for i, groups in enumerate(levels)],
        left_sector,
        destination,
        right_sector,
        left_size,
        sizes,
        slots,
        labels,
        psi,
        left_env,
        right_env.reshape(right_env.shape[:2] + (width // group, group, states)),
    )
    return pl.pallas_call(
        functools.partial(add_kernel, peers, cap),
        out_shape=jax.ShapeDtypeStruct((2, blocks, rows, states), bf16),
        in_specs=[smem, vmem],
        out_specs=vmem,
        scratch_shapes=[pltpu.VMEM((2, blocks, rows, states), f32)],
        compiler_params=pltpu.CompilerParams(vmem_limit_bytes=32 * MIB),
        name="add_targets",
    )(lab_in, landed)


def plain_body(
    psi,
    left_env,
    right_env,
    left_sector,
    right_sector,
    dest_device,
    target_block,
    left_size,
    right_size,
):
    blocks = psi.shape[1]
    width = psi.shape[2]
    states = psi.shape[3]
    peers = lax.axis_size("bond")
    capacity = max(2, 2 * blocks // peers)
    slots = peers * capacity
    rows_all = jnp.arange(states, dtype=jnp.int32)
    left_in = rows_all[None, :] < left_size[:, None]
    masked_left = jnp.where(
        left_in[None, :, :, None] & left_in[None, :, None, :], left_env, jnp.zeros_like(left_env)
    )
    col_rows = lax.axis_index("sub") * width + jnp.arange(width, dtype=jnp.int32)
    right_rows = col_rows[None, :] < right_size[:, None]
    right_cols = rows_all[None, :] < right_size[:, None]
    masked_right = jnp.where(
        right_rows[None, :, :, None] & right_cols[None, :, None, :],
        right_env,
        jnp.zeros_like(right_env),
    )
    left_pieces = masked_left[:, left_sector]
    destination = dest_device[:, 0]
    peer_hits = (destination[:, None] == jnp.arange(peers, dtype=jnp.int32)[None, :]).astype(
        jnp.int32
    )
    earlier = jnp.sum(peer_hits * (jnp.cumsum(peer_hits, axis=0) - peer_hits), axis=1)
    slot_of = destination * capacity + earlier
    block_ids = jnp.arange(blocks, dtype=jnp.int32)
    labels = (
        jnp.zeros((slots, 2), jnp.int32)
        .at[slot_of]
        .set(jnp.stack([target_block, right_sector], axis=1))
    )
    half = jnp.einsum(
        "vkcb,wkab->kvwca", psi, left_pieces, preferred_element_type=jnp.float32
    ).astype(jnp.bfloat16)
    empty = jnp.zeros((slots,) + half.shape[1:], jnp.bfloat16)
    received = lax.all_to_all(
        empty.at[slot_of].set(half), "bond", split_axis=0, concat_axis=0, tiled=True
    )
    labels_in = lax.all_to_all(labels, "bond", split_axis=0, concat_axis=0, tiled=True)
    right_pieces = masked_right[:, labels_in[:, 1]]
    product = jnp.einsum(
        "jvwca,wjcd->vjad", received, right_pieces, preferred_element_type=jnp.float32
    )
    placing = (labels_in[:, 0][:, None] == block_ids[None, :]).astype(jnp.float32)
    partial_sum = jnp.einsum("jt,vjad->vtad", placing, product, precision=lax.Precision.HIGHEST)
    return lax.psum_scatter(partial_sum, ("mpo", "sub"), scatter_dimension=2, tiled=True).astype(
        jnp.bfloat16
    )


def solution(mesh):
    in_specs = (
        P(None, ("grp", "bond"), "sub", None),
        P("mpo", ("grp", "bond"), None, None),
        P("mpo", ("grp", "bond"), "sub", None),
        P(("grp", "bond")),
        P(("grp", "bond")),
        P(("grp", "bond"), None),
        P(("grp", "bond")),
        P(("grp", "bond")),
        P(("grp", "bond")),
    )
    out_specs = P(None, ("grp", "bond"), ("mpo", "sub"), None)
    paired = mesh.shape["mpo"] == 2 and mesh.shape["sub"] == 2
    return jax.shard_map(body if paired else plain_body, mesh=mesh, in_specs=in_specs, out_specs=out_specs, check_vma=False)
```

```python
import functools

import jax
import jax.numpy as jnp
from jax import lax
from jax.experimental import pallas as pl
from jax.experimental.pallas import tpu as pltpu
from jax.sharding import PartitionSpec as P

MESH = pl.DeviceIdType.MESH
MIB = 1024 * 1024
UNROLL = 2
LEVELS = (21, 23, 26)


def contract_kernel(
    peers,
    steps,
    cap,
    groups,
    lsec,
    dest,
    rsec,
    lsize,
    sizes,
    slots,
    labels,
    psi_hbm,
    left_hbm,
    right_hbm,
    landed,
    lab_out,
    psi_v,
    left_v,
    acc,
    send_a,
    recv_a,
    send_b,
    recv_b,
    mine,
    done,
    send_c,
    stage,
    chunks,
    psi_sem,
    left_sem,
    own_sem,
    swap_sem,
    lab_send,
    lab_recv,
    lab_own,
    right_send,
    left_send,
    hop_recv,
    a_sem,
    b_sem,
    c_send,
    c_recv,
    c_own,
    starts,
    order_sector,
    order_part,
    order_size,
):
    me = lax.axis_index("bond")
    m = lax.axis_index("mpo")
    s = lax.axis_index("sub")
    other = {"sub": 1 - s}
    half_w = left_v.shape[0]
    wide = half_w // steps
    width = psi_hbm.shape[2]
    states = psi_hbm.shape[3]
    parts = right_hbm.shape[2]
    spare = chunks[0].shape[2] - groups
    blocks = psi_v.shape[1]
    rows = states // 4

    def remote(src, dst, send_sem, recv_sem, where):
        return pltpu.make_async_remote_copy(
            src_ref=src,
            dst_ref=dst,
            send_sem=send_sem,
            recv_sem=recv_sem,
            device_id=where,
            device_id_type=MESH,
        )

    left_copy = pltpu.make_async_copy(left_hbm.at[pl.ds(s * half_w, half_w)], left_v, left_sem)
    left_copy.start()
    own = []
    for i in range(steps):
        cp = pltpu.make_async_copy(
            right_hbm.at[pl.ds(s * half_w + i * wide, wide)],
            stage[i].at[:, :, pl.ds(s * parts, parts)],
            own_sem.at[i],
        )
        cp.start()
        own.append(cp)
    psi_own = pltpu.make_async_copy(psi_hbm, psi_v.at[:, :, pl.ds(s * width, width)], psi_sem.at[0])
    psi_own.start()

    barrier = pltpu.get_barrier_semaphore()
    pl.semaphore_signal(barrier, inc=1, device_id=other, device_id_type=MESH)
    pl.semaphore_signal(barrier, inc=1, device_id={"mpo": 1 - m}, device_id_type=MESH)
    for delta in range(1, peers):
        pl.semaphore_signal(
            barrier, inc=1, device_id={"bond": lax.rem(me + delta, peers)}, device_id_type=MESH
        )
    pl.semaphore_wait(barrier, peers + 1)

    swaps = []
    for i in range(steps):
        cp = remote(
            right_hbm.at[pl.ds((1 - s) * half_w + i * wide, wide)],
            stage[i].at[:, :, pl.ds(s * parts, parts)],
            swap_sem.at[0, i],
            swap_sem.at[1, i],
            other,
        )
        cp.start()
        swaps.append(cp)
    psi_swap = remote(
        psi_hbm, psi_v.at[:, :, pl.ds(s * width, width)], psi_sem.at[1], psi_sem.at[2], other
    )
    psi_swap.start()

    sectors = right_hbm.shape[1]
    first = lax.axis_index("grp") * peers
    group = right_hbm.shape[3]

    @pl.loop(0, peers)
    def _(p):
        run = 0
        for r in range(sectors):
            starts[p * sectors + r] = run
            run += (sizes[first + p, 0, r] + (group - 1)) // group

    def next_group(g, carry):
        r, part = carry
        safe = jnp.minimum(r, sectors - 1)
        size = sizes[first + me, 0, safe]
        order_sector[g] = safe
        order_part[g] = part
        order_size[g] = jnp.where(r < sectors, size, 0)
        last = (part + 1) * group >= size
        return jnp.where(last, r + 1, r), jnp.where(last, 0, part + 1)

    lax.fori_loop(0, groups, next_group, (jnp.int32(0), jnp.int32(0)))

    lane = lax.broadcasted_iota(jnp.int32, (states, states), 1)
    row = lax.broadcasted_iota(jnp.int32, (states, states), 0)

    def to_right(i, src):
        return remote(
            chunks[i].at[src, :, pl.ds(0, groups)],
            chunks[i].at[src, :, pl.ds(0, groups)],
            right_send.at[i, src],
            hop_recv.at[i, src],
            {"bond": lax.rem(me + 1, peers)},
        )

    def to_left(i, src):
        return remote(
            chunks[i].at[src, :, pl.ds(0, groups)],
            chunks[i].at[src, :, pl.ds(0, groups)],
            left_send.at[i, src],
            hop_recv.at[i, src],
            {"bond": lax.rem(me + peers - 1, peers)},
        )

    for i in range(steps):
        own[i].wait()
        swaps[i].wait_recv()

        @pl.loop(0, groups, unroll=4)
        def _(g):
            keep = jnp.where(lane[:16] < order_size[g], 1.0, 0.0).astype(jnp.bfloat16)
            r = order_sector[g]
            part = order_part[g]
            for w in range(wide):
                chunks[i][me, w, g] = stage[i][w, r, part] * keep

        @pl.when(me < peers - 1)
        def _():
            to_right(i, me).start()

        @pl.when(me > 0)
        def _():
            to_left(i, me).start()

    lab_copies = []
    for delta in range(1, peers):
        q = lax.rem(me + delta, peers)
        cp = remote(labels.at[q], lab_out.at[me], lab_send.at[q], lab_recv.at[me], {"bond": q})
        cp.start()
        lab_copies.append(cp)
    lab_mine = pltpu.make_async_copy(labels.at[me], lab_out.at[me], lab_own)
    lab_mine.start()

    for i in range(steps):
        for p in range(peers):
            chunks[i][p, :, groups:] = jnp.zeros((wide, spare) + chunks[i].shape[3:], jnp.bfloat16)

    psi_own.wait()
    psi_swap.wait()
    left_copy.wait()

    def forward(h, i):
        @pl.when(me - h >= 0)
        def _():
            to_right(i, me - h).wait_recv()

            @pl.when(me < peers - 1)
            def _():
                to_right(i, me - h).start()

        @pl.when(me + h <= peers - 1)
        def _():
            to_left(i, me + h).wait_recv()

            @pl.when(me > 0)
            def _():
                to_left(i, me + h).start()

    def compute(i):
        @pl.loop(0, blocks, unroll=UNROLL)
        def _(k):
            l = lsec[k]
            q = dest[k]
            r = rsec[k]
            start = starts[q * sectors + r]
            inside = (lane < lsize[l]) & (row < sizes[first + q, 0, r])
            keep = jnp.where(inside, 1.0, 0.0).astype(jnp.bfloat16)
            vec = jnp.concatenate([psi_v[0, k] * keep, psi_v[1, k] * keep], axis=0)
            tops, bottoms, pieces = [], [], []
            for w in range(wide):
                out = lax.dot_general(
                    left_v[i * wide + w, l],
                    vec,
                    (((1,), (1,)), ((), ())),
                    preferred_element_type=jnp.float32,
                ).astype(jnp.bfloat16)
                tops.append(out[:, :states])
                bottoms.append(out[:, states:])
                pieces.append(
                    chunks[i][q, w, pl.ds(start, 2 * parts)].reshape(states, states)
                )
            lhs = jnp.concatenate(
                [jnp.concatenate(tops, axis=1), jnp.concatenate(bottoms, axis=1)], axis=0
            )
            rhs = jnp.concatenate(pieces, axis=0)
            total = jnp.dot(lhs, rhs, preferred_element_type=jnp.float32)
            if i == 0:
                acc[k] = total
            else:
                acc[k] += total

    for h in range(1, peers - 1):
        for i in range(steps):
            forward(h, i)
    for i in range(steps):
        forward(peers - 1, i)
        compute(i)

    piece_row = lax.broadcasted_iota(jnp.int32, (rows, states), 0)

    def piece(k, v, mm, ss):
        start = mm * (2 * rows) + ss * rows
        value = acc[k, pl.ds(pl.multiple_of(v * states + start, rows), rows)]
        return jnp.where(piece_row + start < lsize[lsec[k]], value, 0.0)

    def copy_a(v):
        return remote(send_a.at[v], recv_a.at[v], a_sem.at[0, v], a_sem.at[1, v], other)

    def copy_b(v):
        return remote(send_b.at[v], recv_b.at[v], b_sem.at[0, v], b_sem.at[1, v], {"mpo": 1 - m})

    def copy_c(v, q, src):
        return remote(
            send_c.at[q, v], landed.at[src, v], c_send.at[v, q], c_recv.at[v, src], {"bond": q}
        )

    def own_c(v):
        return pltpu.make_async_copy(send_c.at[me, v], landed.at[me, v], c_own.at[v])

    for v in range(2):

        @pl.loop(0, blocks, unroll=2)
        def _(k):
            for mm in range(2):
                send_a[v, k, mm] = piece(k, v, mm, 1 - s).astype(jnp.bfloat16)

        copy_a(v).start()

    for v in range(2):
        copy_a(v).wait_recv()

        @pl.loop(0, blocks, unroll=2)
        def _(k):
            send_b[v, k] = (
                piece(k, v, 1 - m, s) + recv_a[v, k, 1 - m].astype(jnp.float32)
            ).astype(jnp.bfloat16)

        copy_b(v).start()

    for v in range(2):

        @pl.loop(0, blocks, unroll=2)
        def _(k):
            mine[v, k] = piece(k, v, m, s) + recv_a[v, k, m].astype(jnp.float32)

    for v in range(2):
        copy_b(v).wait_recv()

        @pl.loop(0, blocks, unroll=2)
        def _(k):
            done[v][k] = (mine[v, k] + recv_b[v, k].astype(jnp.float32)).astype(jnp.bfloat16)

        for delta in range(1, peers + 1):
            q = lax.rem(me + delta, peers)

            @pl.loop(0, cap, unroll=2)
            def _(j):
                send_c[q, v, j] = done[v][slots[q, 0, j]]

            if delta < peers:
                copy_c(v, q, me).start()
            else:
                own_c(v).start()

    for v in range(2):
        copy_a(v).wait_send()
        copy_b(v).wait_send()
        own_c(v).wait()
        for delta in range(1, peers):
            q = lax.rem(me + delta, peers)
            copy_c(v, q, me).wait_send()
            copy_c(v, q, q).wait_recv()

    for delta in range(1, peers):
        lab_copies[delta - 1].wait_send()
        src = lax.rem(me + peers - delta, peers)
        remote(
            labels.at[src], lab_out.at[src], lab_send.at[src], lab_recv.at[src], {"bond": src}
        ).wait_recv()
    lab_mine.wait()
    for i in range(steps):
        swaps[i].wait_send()
        for h in range(peers):

            @pl.when((me - h >= 0) & (me < peers - 1))
            def _():
                to_right(i, me - h).wait_send()

            @pl.when((me + h <= peers - 1) & (me > 0))
            def _():
                to_left(i, me + h).wait_send()


def add_kernel(peers, cap, labels, landed, out, total):
    total[...] = jnp.zeros_like(total)
    for p in range(peers):

        @pl.loop(0, cap)
        def _(j):
            t = labels[p, 0, j]

            @pl.when(t >= 0)
            def _():
                for v in range(2):
                    total[v, t] += landed[p, v, j].astype(jnp.float32)

    out[...] = total[...].astype(out.dtype)


def share_kernel(
    peers, group, levels, own, dest_col, dest_row, target_col, sizes, slots, labels, level,
    send_sem, recv_sem, own_sem
):
    g, me = lax.axis_index("grp"), lax.axis_index("bond")
    parts = lax.axis_size("grp")
    mine = g * peers + me
    far = [(a, b) for a in range(parts) for b in range(peers) if a or b]

    def place(a, b):
        return lax.rem(g + a, parts), lax.rem(me + b, peers)

    barrier = pltpu.get_barrier_semaphore()
    for a, b in far:
        x, y = place(a, b)
        pl.semaphore_signal(
            barrier, inc=1, device_id={"grp": x, "bond": y}, device_id_type=MESH
        )
    own_copy = pltpu.make_async_copy(own, sizes.at[mine], own_sem)
    own_copy.start()
    pl.semaphore_wait(barrier, len(far))

    def copy(slot, a, b):
        x, y = place(a, b)
        return pltpu.make_async_remote_copy(
            src_ref=own,
            dst_ref=sizes.at[slot],
            send_sem=send_sem.at[x * peers + y],
            recv_sem=recv_sem.at[slot],
            device_id={"grp": x, "bond": y},
            device_id_type=MESH,
        )

    for a, b in far:
        copy(mine, a, b).start()

    blocks = dest_col.shape[0]
    col, line = dest_col[...], dest_row[...]
    ks = lax.broadcasted_iota(jnp.int32, (blocks, blocks), 0)
    js = lax.broadcasted_iota(jnp.int32, (blocks, blocks), 1)
    rank = jnp.sum(jnp.where((col == line) & (js < ks), 1, 0), axis=1, keepdims=True)
    lane = lax.broadcasted_iota(jnp.int32, (blocks, 128), 1)
    ids = lax.broadcasted_iota(jnp.int32, (blocks, 128), 0)
    named = target_col[...] + 1
    for q in range(peers):
        at = (col == q) & (rank == lane)
        slots[q] = jnp.broadcast_to(
            jnp.sum(jnp.where(at, ids, 0), axis=0, keepdims=True), (8, 128)
        )
        labels[q] = jnp.broadcast_to(
            jnp.sum(jnp.where(at, named, 0), axis=0, keepdims=True) - 1, (8, 128)
        )

    own_copy.wait()
    for a, b in far:
        x, y = place(a, b)
        copy(mine, a, b).wait_send()
        copy(x * peers + y, a, b).wait_recv()
    most = jnp.zeros((8, 1), jnp.int32)
    for p in range(parts * peers):
        count = lax.shift_right_logical(sizes[p] + (group - 1), group.bit_length() - 1)
        most = jnp.maximum(most, jnp.sum(count, axis=1, keepdims=True))
    found = jnp.zeros((8, 1), jnp.int32)
    for edge in levels[:-1]:
        found += jnp.where(most > edge, 1, 0)
    level[...] = jnp.broadcast_to(found, (8, 128))


def body(
    psi,
    left_env,
    right_env,
    left_sector,
    right_sector,
    dest_device,
    target_block,
    left_size,
    right_size,
):
    blocks = psi.shape[1]
    width = psi.shape[2]
    states = psi.shape[3]
    sectors = right_env.shape[1]
    half_w = right_env.shape[0] // 2
    peers = lax.axis_size("bond")
    cap = max(2, 2 * blocks // peers)
    steps = 5
    wide = half_w // steps
    rows = states // 4
    destination = dest_device[:, 0]
    smem = pl.BlockSpec(memory_space=pltpu.SMEM)
    vmem = pl.BlockSpec(memory_space=pltpu.VMEM)
    hbm = pl.BlockSpec(memory_space=pl.ANY)
    bf16, f32, i32 = jnp.bfloat16, jnp.float32, jnp.int32
    dma = pltpu.SemaphoreType.DMA
    group = 16
    per = states // group
    total_groups = sectors * per
    levels = [total_groups * f // 32 for f in LEVELS] + [total_groups]
    owners = lax.axis_size("grp") * peers
    own_sizes = jnp.pad(
        jnp.broadcast_to(right_size[None, :], (8, sectors)), ((0, 0), (0, 128 - sectors))
    )
    sizes, slots, labels, level = pl.pallas_call(
        functools.partial(share_kernel, peers, group, levels),
        out_shape=(
            jax.ShapeDtypeStruct((owners, 8, 128), i32),
            jax.ShapeDtypeStruct((peers, 8, 128), i32),
            jax.ShapeDtypeStruct((peers, 8, 128), i32),
            jax.ShapeDtypeStruct((8, 128), i32),
        ),
        in_specs=[vmem] * 4,
        out_specs=(vmem,) * 4,
        scratch_shapes=[dma((owners,)), dma((owners,)), dma],
        compiler_params=pltpu.CompilerParams(collective_id=0, has_side_effects=True),
        name="share_sizes",
    )(own_sizes, dest_device, destination.reshape(1, -1), target_block.reshape(-1, 1))

    def contract(number, groups, *operands):
        return pl.pallas_call(
            functools.partial(contract_kernel, peers, steps, cap, groups),
            out_shape=(
                jax.ShapeDtypeStruct((peers, 2, cap, rows, states), bf16),
                jax.ShapeDtypeStruct((peers, 8, 128), jnp.int32),
            ),
            in_specs=[smem] * 6 + [vmem] + [hbm] * 3,
            out_specs=(hbm, hbm),
            scratch_shapes=[
                pltpu.VMEM((2, blocks, states, states), bf16),
                pltpu.VMEM((half_w, sectors, states, states), bf16),
                pltpu.VMEM((blocks, 2 * states, states), f32),
                pltpu.VMEM((2, blocks, 2, rows, states), bf16),
                pltpu.VMEM((2, blocks, 2, rows, states), bf16),
                pltpu.VMEM((2, blocks, rows, states), bf16),
                pltpu.VMEM((2, blocks, rows, states), bf16),
                pltpu.VMEM((2, blocks, rows, states), f32),
                [pltpu.VMEM((blocks, rows, states), bf16) for _ in range(2)],
                pltpu.VMEM((peers, 2, cap, rows, states), bf16),
                [pltpu.VMEM((wide, sectors, per, group, states), bf16) for _ in range(steps)],
                [
                    pltpu.VMEM((peers, wide, groups + per, group, states), bf16)
                    for _ in range(steps)
                ],
                dma((3,)),
                dma,
                dma((steps,)),
                dma((2, steps)),
                dma((peers,)),
                dma((peers,)),
                dma,
                dma((steps, peers)),
                dma((steps, peers)),
                dma((steps, peers)),
                dma((2, 2)),
                dma((2, 2)),
                dma((2, peers)),
                dma((2, peers)),
                dma((2,)),
                pltpu.SMEM((peers * sectors,), i32),
                pltpu.SMEM((total_groups,), i32),
                pltpu.SMEM((total_groups,), i32),
                pltpu.SMEM((total_groups,), i32),
            ],
            compiler_params=pltpu.CompilerParams(
                collective_id=number + 1, has_side_effects=True, vmem_limit_bytes=60 * MIB
            ),
            name="gather_contract_%d" % groups,
        )(*operands)

    landed, lab_in = lax.switch(
        level[0, 0],
        [functools.partial(contract, i, groups) for i, groups in enumerate(levels)],
        left_sector,
        destination,
        right_sector,
        left_size,
        sizes,
        slots,
        labels,
        psi,
        left_env,
        right_env.reshape(right_env.shape[:2] + (width // group, group, states)),
    )
    return pl.pallas_call(
        functools.partial(add_kernel, peers, cap),
        out_shape=jax.ShapeDtypeStruct((2, blocks, rows, states), bf16),
        in_specs=[smem, vmem],
        out_specs=vmem,
        scratch_shapes=[pltpu.VMEM((2, blocks, rows, states), f32)],
        compiler_params=pltpu.CompilerParams(vmem_limit_bytes=32 * MIB),
        name="add_targets",
    )(lab_in, landed)


def plain_body(
    psi,
    left_env,
    right_env,
    left_sector,
    right_sector,
    dest_device,
    target_block,
    left_size,
    right_size,
):
    blocks = psi.shape[1]
    width = psi.shape[2]
    states = psi.shape[3]
    peers = lax.axis_size("bond")
    capacity = max(2, 2 * blocks // peers)
    slots = peers * capacity
    rows_all = jnp.arange(states, dtype=jnp.int32)
    left_in = rows_all[None, :] < left_size[:, None]
    masked_left = jnp.where(
        left_in[None, :, :, None] & left_in[None, :, None, :], left_env, jnp.zeros_like(left_env)
    )
    col_rows = lax.axis_index("sub") * width + jnp.arange(width, dtype=jnp.int32)
    right_rows = col_rows[None, :] < right_size[:, None]
    right_cols = rows_all[None, :] < right_size[:, None]
    masked_right = jnp.where(
        right_rows[None, :, :, None] & right_cols[None, :, None, :],
        right_env,
        jnp.zeros_like(right_env),
    )
    left_pieces = masked_left[:, left_sector]
    destination = dest_device[:, 0]
    peer_hits = (destination[:, None] == jnp.arange(peers, dtype=jnp.int32)[None, :]).astype(
        jnp.int32
    )
    earlier = jnp.sum(peer_hits * (jnp.cumsum(peer_hits, axis=0) - peer_hits), axis=1)
    slot_of = destination * capacity + earlier
    block_ids = jnp.arange(blocks, dtype=jnp.int32)
    labels = (
        jnp.zeros((slots, 2), jnp.int32)
        .at[slot_of]
        .set(jnp.stack([target_block, right_sector], axis=1))
    )
    half = jnp.einsum(
        "vkcb,wkab->kvwca", psi, left_pieces, preferred_element_type=jnp.float32
    ).astype(jnp.bfloat16)
    empty = jnp.zeros((slots,) + half.shape[1:], jnp.bfloat16)
    received = lax.all_to_all(
        empty.at[slot_of].set(half), "bond", split_axis=0, concat_axis=0, tiled=True
    )
    labels_in = lax.all_to_all(labels, "bond", split_axis=0, concat_axis=0, tiled=True)
    right_pieces = masked_right[:, labels_in[:, 1]]
    product = jnp.einsum(
        "jvwca,wjcd->vjad", received, right_pieces, preferred_element_type=jnp.float32
    )
    placing = (labels_in[:, 0][:, None] == block_ids[None, :]).astype(jnp.float32)
    partial_sum = jnp.einsum("jt,vjad->vtad", placing, product, precision=lax.Precision.HIGHEST)
    return lax.psum_scatter(partial_sum, ("mpo", "sub"), scatter_dimension=2, tiled=True).astype(
        jnp.bfloat16
    )


def solution(mesh):
    in_specs = (
        P(None, ("grp", "bond"), "sub", None),
        P("mpo", ("grp", "bond"), None, None),
        P("mpo", ("grp", "bond"), "sub", None),
        P(("grp", "bond")),
        P(("grp", "bond")),
        P(("grp", "bond"), None),
        P(("grp", "bond")),
        P(("grp", "bond")),
        P(("grp", "bond")),
    )
    out_specs = P(None, ("grp", "bond"), ("mpo", "sub"), None)
    paired = mesh.shape["mpo"] == 2 and mesh.shape["sub"] == 2
    return jax.shard_map(body if paired else plain_body, mesh=mesh, in_specs=in_specs, out_specs=out_specs, check_vma=False)
```
